32 devices in a mesh: frame: 4 (over z), tile: 8 (over y, x, core).
Axes of the slice: x: 2, y: 2, z: 4, core: 2. Of those that a mesh axis runs over, the one named last changes fastest.
Arguments:
- query_tokens: bfloat16 [16, 3072, 1536], P('frame', 'tile'), may hold values from -6 to 6
- key_tokens: bfloat16 [16, 3072, 1536], P('frame', 'tile'), may hold values from -6 to 6
- value_tokens: bfloat16 [16, 3072, 1536], P('frame', 'tile'), may hold values from -6 to 6
- cached_out: bfloat16 [16, 3072, 1536], P('frame', 'tile'), may hold values from -6 to 6
- pattern: int32 [16, 24, 6], P('frame', 'tile'), may hold values from 0 to 1, as said below
- refresh: int32 [16, 24], P('frame', 'tile'), may hold values from 0 to 1, as said below
Outputs:
- refreshed: bfloat16 [16, 3072, 1536], P('frame', 'tile')
The draws below stay inside these ranges and needn't reach their ends.
Inputs may be any that keep to these rules, and one draw needn't show every extreme that they name: `pattern`: entries 0, 1, 2 (a block's left neighbour, itself and its right neighbour in its own frame) are 1. `refresh`: on the blocks of one device (frames t * 4 to t * 4 + 3, spatial blocks s * 3 to s * 3 + 2), the first and the last spatial block of the device's first frame are flagged, at most 9 blocks are flagged, and some device has exactly 9.
All inputs are finite; a program needn't handle non-finite values.
Results may differ from the reference program's by a relative error of at most 0.004.
Values may be sent and summed in bfloat16 or wider, within the bound.
A program may use at most 128 MiB of HBM per device.

```python
import jax
import jax.numpy as jnp
from jax import lax

HEADS = 12
HEAD_DIM = 128
BLK = 128
SB = 3
FR_DEV = 4
CAP = 9
HD = 1536
NF = 16
NS = 3072
N_FRAME = 4
N_TILE = 8


def drawn_parts(key):
    frames_all = FR_DEV * N_FRAME
    tokens_all = SB * N_TILE * BLK
    row_width = HEADS * HEAD_DIM
    full_shape = (frames_all, tokens_all, row_width)
    return full_shape


def draw_query_tokens(key, part):
    full_shape = drawn_parts(key)
    values = jnp.clip(jax.random.normal(jax.random.fold_in(key, 1), full_shape, jnp.float32), -6.0, 6.0)
    return values.astype(jnp.bfloat16)


def draw_key_tokens(key, part):
    full_shape = drawn_parts(key)
    values = jnp.clip(jax.random.normal(jax.random.fold_in(key, 2), full_shape, jnp.float32), -6.0, 6.0)
    return values.astype(jnp.bfloat16)


def draw_pattern(key, part):
    frames_all = FR_DEV * N_FRAME
    blocks_all = SB * N_TILE
    coins = jax.random.randint(jax.random.fold_in(key, 5), (frames_all, blocks_all, 6), 0, 4)
    neighbour = lax.broadcasted_iota(jnp.int32, (frames_all, blocks_all, 6), 2)
    return jnp.where((neighbour < 3) | (coins > 0), 1, 0).astype(jnp.int32)


def draw_refresh(key, part):
    per_device = FR_DEV * SB
    devices_all = N_FRAME * N_TILE
    counts = jax.random.randint(jax.random.fold_in(key, 21), (devices_all,), 2, CAP + 1)
    busiest = jax.random.randint(jax.random.fold_in(key, 22), (), 0, devices_all)
    counts = jnp.where(jnp.arange(devices_all, dtype=jnp.int32) == busiest, CAP, counts)
    counts = counts.reshape(N_FRAME, N_TILE, 1)
    random_part = jax.random.randint(jax.random.fold_in(key, 23), (N_FRAME, N_TILE, per_device), 0, 1 << 20)
    local_ids = jnp.arange(per_device, dtype=jnp.int32)
    scores = random_part * per_device + local_ids
    frame_of = local_ids // SB
    block_of = local_ids % SB
    forced = (frame_of == 0) & ((block_of == 0) | (block_of == SB - 1))
    scores = jnp.where(forced, -1 - local_ids, scores)
    sorting = jnp.argsort(scores, axis=-1, stable=True)
    ranking = jnp.argsort(sorting, axis=-1, stable=True)
    flag_rows = (ranking < counts).astype(jnp.int32)
    flag_rows = flag_rows.reshape(N_FRAME, N_TILE, FR_DEV, SB).transpose(0, 2, 1, 3)
    return flag_rows.reshape(N_FRAME * FR_DEV, N_TILE * SB)


def shard_levels(own_key, extent, split, least, top_value):
    level = 1.0
    for position, blocks in split:
        steps = jax.random.uniform(jax.random.fold_in(jax.random.fold_in(own_key, 6), position), (blocks,), jnp.float32, least / len(split), top_value / len(split))
        level = level * jnp.repeat(jnp.exp(steps), extent[position] // blocks).reshape((-1,) + (1,) * (len(extent) - 1 - position))
    return level


def bell_draw(key, shape, scale, limit, cuts=(), kind=jnp.bfloat16):
    result = jax.random.normal(key, shape, jnp.float32) * scale
    if len(cuts) > 0:
        result = shard_levels(key, shape, cuts, -0.22, 0.18) * result
    return jnp.clip(result, min=-limit, max=limit).astype(kind)


def setup_inputs(seed: int = 0) -> dict:
    arg_keys = jax.random.split(jax.random.key(seed), 7)
    query_tokens = draw_query_tokens(jax.random.fold_in(arg_keys[6], 71), 0)
    key_tokens = draw_key_tokens(jax.random.fold_in(arg_keys[6], 71), 0)
    value_tokens = bell_draw(arg_keys[2], (NF, NS, HD), 1.0, 6.0, ((0, 4), (1, 8)))
    cached_out = bell_draw(arg_keys[3], (NF, NS, HD), 1.0, 6.0, ((0, 4), (1, 8)))
    pattern = draw_pattern(jax.random.fold_in(arg_keys[6], 71), 0)
    refresh = draw_refresh(jax.random.fold_in(arg_keys[6], 71), 0)
    return {"query_tokens": query_tokens, "key_tokens": key_tokens, "value_tokens": value_tokens, "cached_out": cached_out, "pattern": pattern, "refresh": refresh}


def attend_rows(query_rows, key_rows, value_rows, allowed):
    block_count = query_rows.shape[0]
    queries_h = query_rows.astype(jnp.float32).reshape(block_count, BLK, HEADS, HEAD_DIM)
    keys_h = key_rows.astype(jnp.float32).reshape(block_count, 6 * BLK, HEADS, HEAD_DIM)
    values_h = value_rows.astype(jnp.float32).reshape(block_count, 6 * BLK, HEADS, HEAD_DIM)
    scores = jnp.einsum("bqhe,bkhe->bhqk", queries_h, keys_h) * (HEAD_DIM ** -0.5)
    key_mask = jnp.repeat(allowed > 0, BLK, axis=1)
    scores = jnp.where(key_mask[:, None, None, :], scores, -jnp.inf)
    row_max = jnp.max(scores, axis=-1, keepdims=True)
    exponentials = jnp.exp(scores - row_max)
    weights = (exponentials / jnp.sum(exponentials, axis=-1, keepdims=True)).astype(jnp.bfloat16)
    attended = jnp.einsum("bhqk,bkhe->bqhe", weights.astype(jnp.float32), values_h)
    return attended.reshape(block_count, BLK, HEADS * HEAD_DIM).astype(jnp.bfloat16)


def reference(query_tokens, key_tokens, value_tokens, cached_out, pattern, refresh):
    frames_all, tokens_all, row_width = query_tokens.shape
    blocks_all = tokens_all // BLK
    joined = jnp.concatenate([key_tokens, value_tokens], axis=2)
    padded = jnp.pad(joined, ((1, 0), (BLK, BLK), (0, 0)))
    padded = padded.reshape(frames_all + 1, blocks_all + 2, BLK, 2 * row_width)
    block_ids = jnp.arange(blocks_all, dtype=jnp.int32)
    neighbour = jnp.arange(6, dtype=jnp.int32)
    offsets = neighbour % 3 - 1
    frame_lags = neighbour // 3

    def one_frame(frame_index):
        windows = []
        for frames_back in (0, 1):
            frame_plane = lax.dynamic_index_in_dim(padded, frame_index + 1 - frames_back, 0, keepdims=False)
            windows.append(jnp.concatenate([frame_plane[0:blocks_all], frame_plane[1:blocks_all + 1], frame_plane[2:blocks_all + 2]], axis=1))
        gathered = jnp.concatenate(windows, axis=1)
        pattern_rows = lax.dynamic_index_in_dim(pattern, frame_index, 0, keepdims=False)
        spatial = block_ids[:, None] + offsets[None, :]
        inside = ((frame_index - frame_lags)[None, :] >= 0) & (spatial >= 0) & (spatial < blocks_all)
        allowed = jnp.where(inside, pattern_rows, 0)
        query_rows = lax.dynamic_index_in_dim(query_tokens, frame_index, 0, keepdims=False).reshape(blocks_all, BLK, row_width)
        attended = attend_rows(query_rows, gathered[..., :row_width], gathered[..., row_width:], allowed)
        cached_rows = lax.dynamic_index_in_dim(cached_out, frame_index, 0, keepdims=False).reshape(blocks_all, BLK, row_width)
        flag_rows = lax.dynamic_index_in_dim(refresh, frame_index, 0, keepdims=False)
        return jnp.where(flag_rows[:, None, None] > 0, attended, cached_rows).reshape(tokens_all, row_width)

    return lax.map(one_frame, jnp.arange(frames_all, dtype=jnp.int32))
```

```python
import functools
import math

import jax
import jax.numpy as jnp
from jax import lax
from jax.experimental import pallas as pl
from jax.experimental.pallas import tpu as pltpu
from jax.sharding import PartitionSpec as P

HEAD_DIM = 128
BLK = 128
GROUP = 3


def shift(block, axis, distance):
    count = lax.axis_size(axis)
    pairs = [(i, i + distance) for i in range(count) if 0 <= i + distance < count]
    return lax.ppermute(block, axis, pairs)


def frame_body(frame, blocks, heads, allow_ref, flag_ref, q_ref, cached_ref, *refs):
    kc, vc, kp, vp, klc, vlc, krc, vrc, klp, vlp, krp, vrp = refs[:12]
    out_ref = refs[-1]
    current = (klc, kc, krc), (vlc, vc, vrc)
    previous = (klp, kp, krp), (vlp, vp, vrp)
    scale2 = math.log2(math.e) * HEAD_DIM ** (-0.5)
    ones = jnp.ones((BLK, HEAD_DIM), jnp.bfloat16)

    def piece(sides, column, cols):
        left, own, right = sides
        if column < 0:
            return left[..., cols].reshape(BLK, HEAD_DIM)
        if column >= blocks:
            return right[..., cols].reshape(BLK, HEAD_DIM)
        return own[..., column * BLK : (column + 1) * BLK, cols].reshape(BLK, HEAD_DIM)

    for b in range(blocks):
        rows = slice(b * BLK, (b + 1) * BLK)
        flagged = flag_ref[frame, b] > 0

        @pl.when(flagged)
        def _():
            allowed = [allow_ref[frame, b * 6 + n] > 0 for n in range(6)]
            for h in range(heads):
                cols = slice(h * HEAD_DIM, (h + 1) * HEAD_DIM)
                query = q_ref[0, rows, cols]
                scores = []
                top = None
                for n in range(6):
                    keys = piece((current, previous)[n // 3][0], b + n % 3 - 1, cols)
                    s = lax.dot_general(
                        query, keys, (((1,), (1,)), ((), ())), preferred_element_type=jnp.float32
                    )
                    scores.append(s)
                    t = s if n == 1 else s + jnp.where(allowed[n], 0.0, -jnp.inf)
                    top = t if top is None else jnp.maximum(top, t)
                row_top = jnp.max(top, axis=1, keepdims=True) * scale2
                weights = []
                values = []
                for n in range(6):
                    base = row_top if n == 1 else row_top + jnp.where(allowed[n], 0.0, jnp.inf)
                    weights.append(jnp.exp2(scores[n] * scale2 - base).astype(jnp.bfloat16))
                    part = piece((current, previous)[n // 3][1], b + n % 3 - 1, cols)
                    values.append(jnp.concatenate([part, ones], axis=1))
                total = jnp.dot(
                    jnp.concatenate(weights, axis=1),
                    jnp.concatenate(values, axis=0),
                    preferred_element_type=jnp.float32,
                )
                out_ref[0, rows, cols] = (total[:, :HEAD_DIM] / total[:, HEAD_DIM:]).astype(out_ref.dtype)

        @pl.when(jnp.logical_not(flagged))
        def _():
            out_ref[0, rows, :] = cached_ref[0, rows, :]


def attend_frame(frame, q, k, v, cached, allowed, flags, halos, behind, out):
    frames, tokens, width = q.shape
    blocks = tokens // BLK
    group = GROUP if (width // HEAD_DIM) % GROUP == 0 else 1
    gw = group * HEAD_DIM

    def whole(f):
        return pl.BlockSpec((1, tokens, gw), lambda g: (f, 0, g))

    def pair(kv, f, n):
        return pl.BlockSpec((1, 1, n, gw), lambda g: (kv, f, 0, g))

    smem = pl.BlockSpec(memory_space=pltpu.SMEM)
    args = [allowed, flags, q, cached, k, v]
    specs = [smem, smem, whole(frame), whole(frame), whole(frame), whole(frame)]
    if frame > 0:
        args += [k, v]
        specs += [whole(frame - 1), whole(frame - 1)]
        rims = [halos[frame], halos[frame - 1]]
    else:
        prev, prev_rims = behind
        args += [prev, prev]
        specs += [pair(0, 0, tokens), pair(1, 0, tokens)]
        rims = [halos[frame], prev_rims]
    for left, right, place in rims:
        args += [left, left, right, right]
        specs += [pair(0, place, BLK), pair(1, place, BLK)] * 2
    aliases = {}
    if out is not None:
        aliases = {len(args): 0}
        args.append(out)
        specs.append(pl.BlockSpec(memory_space=pl.ANY))
    work = 4 * tokens * 6 * BLK * width
    return pl.pallas_call(
        functools.partial(frame_body, frame, blocks, group),
        grid=(width // gw,),
        in_specs=specs,
        out_specs=whole(frame),
        out_shape=jax.ShapeDtypeStruct(q.shape, q.dtype),
        input_output_aliases=aliases,
        compiler_params=pltpu.CompilerParams(vmem_limit_bytes=40 << 20),
        cost_estimate=pl.CostEstimate(
            flops=4 * work, bytes_accessed=12 * tokens * width * 2, transcendentals=0
        ),
        name=f"attend_frame_{frame}",
    )(*args)


def local(q, k, v, cached, pattern, refresh):
    frames, tokens, width = q.shape
    blocks = tokens // BLK
    last = frames - 1

    frame_at = lax.axis_index("frame") * frames + jnp.arange(frames, dtype=jnp.int32)
    block_at = lax.axis_index("tile") * blocks + jnp.arange(blocks, dtype=jnp.int32)
    n = jnp.arange(6, dtype=jnp.int32)
    spatial = block_at[None, :, None] + (n % 3 - 1)[None, None, :]
    inside = (
        (frame_at[:, None, None] - (n // 3)[None, None, :] >= 0)
        & (spatial >= 0)
        & (spatial < blocks * lax.axis_size("tile"))
    )
    allowed = jnp.where(inside, pattern, 0).reshape(frames, blocks * 6)

    prev = shift(jnp.stack([k[last:], v[last:]]), "frame", 1)
    halos = [None] * frames
    half = max(frames // 2, 1)
    starts = list(range(0, frames, half))[::-1]
    for start in starts:
        stop = min(start + half, frames)
        tail = jnp.stack([k[start:stop, tokens - BLK :], v[start:stop, tokens - BLK :]])
        head = jnp.stack([k[start:stop, :BLK], v[start:stop, :BLK]])
        left = shift(tail, "tile", 1)
        right = shift(head, "tile", -1)
        for f in range(start, stop):
            halos[f] = (left, right, f - start)
    prev_left = shift(prev[:, :, tokens - BLK :], "tile", 1)
    prev_right = shift(prev[:, :, :BLK], "tile", -1)
    behind = (prev, (prev_left, prev_right, 0))

    out = None
    for frame in range(frames - 1, -1, -1):
        out = attend_frame(frame, q, k, v, cached, allowed, refresh, halos, behind, out)
    return out


def solution(mesh):
    wide = P("frame", "tile", None)
    return jax.shard_map(
        local,
        mesh=mesh,
        in_specs=(wide, wide, wide, wide, wide, P("frame", "tile")),
        out_specs=wide,
        check_vma=False,
    )
```

```python
import functools
import math

import jax
import jax.numpy as jnp
from jax import lax
from jax.experimental import pallas as pl
from jax.experimental.pallas import tpu as pltpu
from jax.sharding import PartitionSpec as P

HEAD_DIM = 128
BLK = 128
GROUP = 6
ROW = 4


def shift(block, axis, distance, skip=lambda i, j: False):
    count = lax.axis_size(axis)
    pairs = [(i, i + distance) for i in range(count) if 0 <= i + distance < count]
    return lax.ppermute(block, axis, [p for p in pairs if not skip(*p)])


def relayed_rims(tail, head):
    count = lax.axis_size("tile")
    if count % ROW or count == ROW:
        return shift(tail, "tile", 1), shift(head, "tile", -1)
    place = lax.axis_index("tile") % ROW
    ups = range(ROW - 1, count - 1, ROW)
    first = [(i, i + ROW) for i in ups] + [(i + 1, i + 1 - ROW) for i in ups]
    second = [(i + ROW, i + 1) for i in ups] + [(i + 1 - ROW, i) for i in ups]
    relay = lax.ppermute(jnp.where(place == 0, head, tail), "tile", first)
    crosses = lambda i, j: i // ROW != j // ROW
    left = shift(tail, "tile", 1, crosses)
    right = shift(head, "tile", -1, crosses)
    relay = lax.ppermute(relay, "tile", second)
    return jnp.where(place == 0, relay, left), jnp.where(place == ROW - 1, relay, right)


def frame_body(frame, blocks, heads, allow_ref, flag_ref, q_ref, cached_ref, *refs):
    kc, vc, kp, vp, klc, vlc, krc, vrc, klp, vlp, krp, vrp = refs[:12]
    out_ref = refs[-1]
    current = (klc, kc, krc), (vlc, vc, vrc)
    previous = (klp, kp, krp), (vlp, vp, vrp)
    scale2 = math.log2(math.e) * HEAD_DIM ** (-0.5)
    ones = jnp.ones((BLK, HEAD_DIM), jnp.bfloat16)

    def piece(sides, column, cols):
        left, own, right = sides
        if column < 0:
            return left[..., cols].reshape(BLK, HEAD_DIM)
        if column >= blocks:
            return right[..., cols].reshape(BLK, HEAD_DIM)
        return own[..., column * BLK : (column + 1) * BLK, cols].reshape(BLK, HEAD_DIM)

    def neighbours(part, column, cols):
        pairs = [(current, previous)[n // 3][part] for n in range(6)]
        return [piece(pairs[n], column + n % 3 - 1, cols) for n in range(6)]

    for b in range(blocks):
        rows = slice(b * BLK, (b + 1) * BLK)
        flagged = flag_ref[frame, b] > 0

        @pl.when(flagged)
        def _():
            bias = [jnp.where(allow_ref[frame, b * 6 + n] > 0, 0.0, -jnp.inf) for n in range(6)]
            columns = [slice(h * HEAD_DIM, (h + 1) * HEAD_DIM) for h in range(heads)]
            scores = []
            for cols in columns:
                s = lax.dot_general(
                    q_ref[0, rows, cols],
                    jnp.concatenate(neighbours(0, b, cols), axis=0),
                    (((1,), (1,)), ((), ())),
                    preferred_element_type=jnp.float32,
                )
                parts = [s[:, n * BLK : (n + 1) * BLK] for n in range(6)]
                scores.append([t if n == 1 else t + bias[n] for n, t in enumerate(parts)])
            weights = []
            for parts in scores:
                top = jnp.max(functools.reduce(jnp.maximum, parts), axis=1, keepdims=True)
                top = jnp.broadcast_to(top * scale2, (BLK, BLK))
                weights.append([jnp.exp2(t * scale2 - top).astype(jnp.bfloat16) for t in parts])
            results = []
            for cols, parts in zip(columns, weights):
                values = [jnp.concatenate([x, ones], axis=1) for x in neighbours(1, b, cols)]
                total = jnp.dot(
                    jnp.concatenate(parts, axis=1),
                    jnp.concatenate(values, axis=0),
                    preferred_element_type=jnp.float32,
                )
                results.append((total[:, :HEAD_DIM] / total[:, HEAD_DIM:]).astype(out_ref.dtype))
            for cols, result in zip(columns, results):
                out_ref[0, rows, cols] = result

        @pl.when(jnp.logical_not(flagged))
        def _():
            out_ref[0, rows, :] = cached_ref[0, rows, :]


def attend_frame(frame, q, k, v, cached, allowed, flags, halos, behind, out):
    frames, tokens, width = q.shape
    blocks = tokens // BLK
    group = math.gcd(width // HEAD_DIM, GROUP)
    gw = group * HEAD_DIM

    def whole(f):
        return pl.BlockSpec((1, tokens, gw), lambda g: (f, 0, g))

    def pair(kv, f, n):
        return pl.BlockSpec((1, 1, n, gw), lambda g: (kv, f, 0, g))

    smem = pl.BlockSpec(memory_space=pltpu.SMEM)
    args = [allowed, flags, q, cached, k, v]
    specs = [smem, smem, whole(frame), whole(frame), whole(frame), whole(frame)]
    if frame > 0:
        args += [k, v]
        specs += [whole(frame - 1), whole(frame - 1)]
        rims = [halos[frame], halos[frame - 1]]
    else:
        prev, prev_rims = behind
        args += [prev, prev]
        specs += [pair(0, 0, tokens), pair(1, 0, tokens)]
        rims = [halos[frame], prev_rims]
    for left, right, place in rims:
        args += [left, left, right, right]
        specs += [pair(0, place, BLK), pair(1, place, BLK)] * 2
    aliases = {}
    if out is not None:
        aliases = {len(args): 0}
        args.append(out)
        specs.append(pl.BlockSpec(memory_space=pl.ANY))
    work = 4 * tokens * 6 * BLK * width
    return pl.pallas_call(
        functools.partial(frame_body, frame, blocks, group),
        grid=(width // gw,),
        in_specs=specs,
        out_specs=whole(frame),
        out_shape=jax.ShapeDtypeStruct(q.shape, q.dtype),
        input_output_aliases=aliases,
        compiler_params=pltpu.CompilerParams(vmem_limit_bytes=60 << 20),
        cost_estimate=pl.CostEstimate(
            flops=4 * work, bytes_accessed=12 * tokens * width * 2, transcendentals=0
        ),
        name=f"attend_frame_{frame}",
    )(*args)


def local(q, k, v, cached, pattern, refresh):
    frames, tokens, width = q.shape
    blocks = tokens // BLK
    last = frames - 1

    frame_at = lax.axis_index("frame") * frames + jnp.arange(frames, dtype=jnp.int32)
    block_at = lax.axis_index("tile") * blocks + jnp.arange(blocks, dtype=jnp.int32)
    n = jnp.arange(6, dtype=jnp.int32)
    spatial = block_at[None, :, None] + (n % 3 - 1)[None, None, :]
    inside = (
        (frame_at[:, None, None] - (n // 3)[None, None, :] >= 0)
        & (spatial >= 0)
        & (spatial < blocks * lax.axis_size("tile"))
    )
    allowed = jnp.where(inside, pattern, 0).reshape(frames, blocks * 6)

    prev = shift(jnp.stack([k[last:], v[last:]]), "frame", 1)
    halos = [None] * frames
    half = max(frames // 2, 1)
    starts = list(range(0, frames, half))[::-1]
    for start in starts:
        stop = min(start + half, frames)
        tail = jnp.stack([k[start:stop, tokens - BLK :], v[start:stop, tokens - BLK :]])
        head = jnp.stack([k[start:stop, :BLK], v[start:stop, :BLK]])
        if start == 0:
            left, right = relayed_rims(tail, head)
        else:
            left, right = shift(tail, "tile", 1), shift(head, "tile", -1)
        for f in range(start, stop):
            halos[f] = (left, right, f - start)
    prev_left = shift(prev[:, :, tokens - BLK :], "tile", 1)
    prev_right = shift(prev[:, :, :BLK], "tile", -1)
    behind = (prev, (prev_left, prev_right, 0))

    out = None
    for frame in range(frames - 1, -1, -1):
        out = attend_frame(frame, q, k, v, cached, allowed, refresh, halos, behind, out)
    return out


def solution(mesh):
    wide = P("frame", "tile", None)
    return jax.shard_map(
        local,
        mesh=mesh,
        in_specs=(wide, wide, wide, wide, wide, P("frame", "tile")),
        out_specs=wide,
        check_vma=False,
    )
```

```python
import functools
import math

import jax
import jax.numpy as jnp
from jax import lax
from jax.experimental import pallas as pl
from jax.experimental.pallas import tpu as pltpu
from jax.sharding import PartitionSpec as P

HEAD_DIM = 128
BLK = 128
GROUP = 6
ROW = 4


def shift(block, axis, distance, skip=lambda i, j: False):
    count = lax.axis_size(axis)
    pairs = [(i, i + distance) for i in range(count) if 0 <= i + distance < count]
    return lax.ppermute(block, axis, [p for p in pairs if not skip(*p)])


def relayed_rims(tail, head):
    count = lax.axis_size("tile")
    if count % ROW or count == ROW:
        return shift(tail, "tile", 1), shift(head, "tile", -1)
    place = lax.axis_index("tile") % ROW
    ups = range(ROW - 1, count - 1, ROW)
    first = [(i, i + ROW) for i in ups] + [(i + 1, i + 1 - ROW) for i in ups]
    second = [(i + ROW, i + 1) for i in ups] + [(i + 1 - ROW, i) for i in ups]
    relay = lax.ppermute(jnp.where(place == 0, head, tail), "tile", first)
    crosses = lambda i, j: i // ROW != j // ROW
    left = shift(tail, "tile", 1, crosses)
    right = shift(head, "tile", -1, crosses)
    relay = lax.ppermute(relay, "tile", second)
    return jnp.where(place == 0, relay, left), jnp.where(place == ROW - 1, relay, right)


def frame_body(frame, blocks, heads, allow_ref, flag_ref, q_ref, cached_ref, *refs):
    own = refs[0], refs[1]
    if frame > 0:
        before, rims = (refs[2], refs[3]), refs[4:8]
    else:
        before, rims = (refs[2].at[0], refs[2].at[1]), refs[3:7]
    out_ref = refs[-1]
    current = [(rims[0].at[i], own[i], rims[1].at[i]) for i in range(2)]
    previous = [(rims[2].at[i], before[i], rims[3].at[i]) for i in range(2)]
    scale2 = math.log2(math.e) * HEAD_DIM ** (-0.5)
    ones = jnp.ones((BLK, HEAD_DIM), jnp.bfloat16)

    def piece(sides, column, cols):
        left, own, right = sides
        if column < 0:
            return left[..., cols].reshape(BLK, HEAD_DIM)
        if column >= blocks:
            return right[..., cols].reshape(BLK, HEAD_DIM)
        return own[..., column * BLK : (column + 1) * BLK, cols].reshape(BLK, HEAD_DIM)

    def neighbours(part, column, cols):
        pairs = [(current, previous)[n // 3][part] for n in range(6)]
        return [piece(pairs[n], column + n % 3 - 1, cols) for n in range(6)]

    for b in range(blocks):
        rows = slice(b * BLK, (b + 1) * BLK)
        flagged = flag_ref[frame, b] > 0

        @pl.when(flagged)
        def _():
            bias = [jnp.where(allow_ref[frame, b * 6 + n] > 0, 0.0, -jnp.inf) for n in range(6)]
            columns = [slice(h * HEAD_DIM, (h + 1) * HEAD_DIM) for h in range(heads)]
            scores = []
            for cols in columns:
                s = lax.dot_general(
                    q_ref[0, rows, cols],
                    jnp.concatenate(neighbours(0, b, cols), axis=0),
                    (((1,), (1,)), ((), ())),
                    preferred_element_type=jnp.float32,
                )
                parts = [s[:, n * BLK : (n + 1) * BLK] for n in range(6)]
                scores.append([t if n == 1 else t + bias[n] for n, t in enumerate(parts)])
            weights = []
            for parts in scores:
                top = jnp.max(functools.reduce(jnp.maximum, parts), axis=1, keepdims=True)
                top = jnp.broadcast_to(top * scale2, (BLK, BLK))
                weights.append([jnp.exp2(t * scale2 - top).astype(jnp.bfloat16) for t in parts])
            results = []
            for cols, parts in zip(columns, weights):
                values = [jnp.concatenate([x, ones], axis=1) for x in neighbours(1, b, cols)]
                total = jnp.dot(
                    jnp.concatenate(parts, axis=1),
                    jnp.concatenate(values, axis=0),
                    preferred_element_type=jnp.float32,
                )
                results.append((total[:, :HEAD_DIM] / total[:, HEAD_DIM:]).astype(out_ref.dtype))
            for cols, result in zip(columns, results):
                out_ref[0, rows, cols] = result

        @pl.when(jnp.logical_not(flagged))
        def _():
            out_ref[0, rows, :] = cached_ref[0, rows, :]


def attend_frame(frame, q, k, v, cached, allowed, flags, halos, behind, out):
    frames, tokens, width = q.shape
    blocks = tokens // BLK
    group = math.gcd(width // HEAD_DIM, GROUP)
    gw = group * HEAD_DIM

    def whole(f):
        return pl.BlockSpec((1, tokens, gw), lambda g: (f, 0, g))

    def pair(f, n):
        return pl.BlockSpec((2, 1, n, gw), lambda g: (0, f, 0, g))

    smem = pl.BlockSpec(memory_space=pltpu.SMEM)
    args = [allowed, flags, q, cached, k, v]
    specs = [smem, smem, whole(frame), whole(frame), whole(frame), whole(frame)]
    if frame > 0:
        args += [k, v]
        specs += [whole(frame - 1), whole(frame - 1)]
        rims = [halos[frame], halos[frame - 1]]
    else:
        prev, prev_rims = behind
        args.append(prev)
        specs.append(pair(0, tokens))
        rims = [halos[frame], prev_rims]
    for left, right, place in rims:
        args += [left, right]
        specs += [pair(place, BLK)] * 2
    aliases = {}
    if out is not None:
        aliases = {len(args): 0}
        args.append(out)
        specs.append(pl.BlockSpec(memory_space=pl.ANY))
    work = 4 * tokens * 6 * BLK * width
    return pl.pallas_call(
        functools.partial(frame_body, frame, blocks, group),
        grid=(width // gw,),
        in_specs=specs,
        out_specs=whole(frame),
        out_shape=jax.ShapeDtypeStruct(q.shape, q.dtype),
        input_output_aliases=aliases,
        compiler_params=pltpu.CompilerParams(vmem_limit_bytes=63 << 20),
        cost_estimate=pl.CostEstimate(
            flops=4 * work, bytes_accessed=12 * tokens * width * 2, transcendentals=0
        ),
        name=f"attend_frame_{frame}",
    )(*args)


def local(q, k, v, cached, pattern, refresh):
    frames, tokens, width = q.shape
    blocks = tokens // BLK
    last = frames - 1

    frame_at = lax.axis_index("frame") * frames + jnp.arange(frames, dtype=jnp.int32)
    block_at = lax.axis_index("tile") * blocks + jnp.arange(blocks, dtype=jnp.int32)
    n = jnp.arange(6, dtype=jnp.int32)
    spatial = block_at[None, :, None] + (n % 3 - 1)[None, None, :]
    inside = (
        (frame_at[:, None, None] - (n // 3)[None, None, :] >= 0)
        & (spatial >= 0)
        & (spatial < blocks * lax.axis_size("tile"))
    )
    allowed = jnp.where(inside, pattern, 0).reshape(frames, blocks * 6)

    prev = shift(jnp.stack([k[last:], v[last:]]), "frame", 1)
    halos = [None] * frames
    half = max(frames // 2, 1)
    starts = list(range(0, frames, half))[::-1]
    for start in starts:
        stop = min(start + half, frames)
        tail = jnp.stack([k[start:stop, tokens - BLK :], v[start:stop, tokens - BLK :]])
        head = jnp.stack([k[start:stop, :BLK], v[start:stop, :BLK]])
        if start == 0:
            left, right = relayed_rims(tail, head)
        else:
            left, right = shift(tail, "tile", 1), shift(head, "tile", -1)
        for f in range(start, stop):
            halos[f] = (left, right, f - start)
    prev_left = shift(prev[:, :, tokens - BLK :], "tile", 1)
    prev_right = shift(prev[:, :, :BLK], "tile", -1)
    behind = (prev, (prev_left, prev_right, 0))

    out = None
    for frame in range(frames - 1, -1, -1):
        out = attend_frame(frame, q, k, v, cached, allowed, refresh, halos, behind, out)
    return out


def solution(mesh):
    wide = P("frame", "tile", None)
    return jax.shard_map(
        local,
        mesh=mesh,
        in_specs=(wide, wide, wide, wide, wide, P("frame", "tile")),
        out_specs=wide,
        check_vma=False,
    )
```

```python
import functools
import math

import jax
import jax.numpy as jnp
from jax import lax
from jax.experimental import pallas as pl
from jax.experimental.pallas import tpu as pltpu
from jax.sharding import PartitionSpec as P

HEAD_DIM = 128
BLK = 128
GROUP = 6
ROW = 4


def shift(block, axis, distance, skip=lambda i, j: False):
    count = lax.axis_size(axis)
    pairs = [(i, i + distance) for i in range(count) if 0 <= i + distance < count]
    return lax.ppermute(block, axis, [p for p in pairs if not skip(*p)])


def relayed_rims(tail, head):
    count = lax.axis_size("tile")
    if count % ROW or count == ROW:
        return shift(tail, "tile", 1), shift(head, "tile", -1), None
    place = lax.axis_index("tile") % ROW
    ups = range(ROW - 1, count - 1, ROW)
    first = [(i, i + ROW) for i in ups] + [(i + 1, i + 1 - ROW) for i in ups]
    second = [(i + ROW, i + 1) for i in ups] + [(i + 1 - ROW, i) for i in ups]
    relay = lax.ppermute(jnp.where(place == 0, head, tail), "tile", first)
    crosses = lambda i, j: i // ROW != j // ROW
    left = shift(tail, "tile", 1, crosses)
    right = shift(head, "tile", -1, crosses)
    relay = lax.ppermute(relay, "tile", second)
    return left, right, relay


def frame_body(frame, relayed, blocks, heads, allow_ref, flag_ref, side_ref, q_ref, cached_ref, *refs):
    own = refs[0], refs[1]
    refs = refs[2:]
    if frame > 0:
        before, refs = (refs[0], refs[1]), refs[2:]
    else:
        before, refs = (refs[0].at[0], refs[0].at[1]), refs[1:]
    out_ref = refs[-1]
    sides = []
    for tokens, by_relay in zip((own, before), relayed):
        left, right = refs[:2]
        relay = refs[2] if by_relay else None
        refs = refs[3 if by_relay else 2 :]
        sides.append(
            [(left.at[i], tokens[i], right.at[i], relay.at[i] if by_relay else None) for i in range(2)]
        )
    current, previous = sides
    scale2 = math.log2(math.e) * HEAD_DIM ** (-0.5)
    ones = jnp.ones((BLK, HEAD_DIM), jnp.bfloat16)

    def piece(sides, column, cols):
        left, own, right, relay = sides
        if 0 <= column < blocks:
            return own[..., column * BLK : (column + 1) * BLK, cols].reshape(BLK, HEAD_DIM)
        direct = (left if column < 0 else right)[..., cols].reshape(BLK, HEAD_DIM)
        if relay is None:
            return direct
        hopped = relay[..., cols].reshape(BLK, HEAD_DIM)
        return lax.select(side_ref[int(column >= 0)] > 0, hopped, direct)

    def neighbours(part, column, cols):
        pairs = [(current, previous)[n // 3][part] for n in range(6)]
        return [piece(pairs[n], column + n % 3 - 1, cols) for n in range(6)]

    for b in range(blocks):
        rows = slice(b * BLK, (b + 1) * BLK)
        flagged = flag_ref[frame, b] > 0

        @pl.when(flagged)
        def _():
            bias = [jnp.where(allow_ref[frame, b * 6 + n] > 0, 0.0, -jnp.inf) for n in range(6)]
            columns = [slice(h * HEAD_DIM, (h + 1) * HEAD_DIM) for h in range(heads)]
            scores = []
            for cols in columns:
                s = lax.dot_general(
                    q_ref[0, rows, cols],
                    jnp.concatenate(neighbours(0, b, cols), axis=0),
                    (((1,), (1,)), ((), ())),
                    preferred_element_type=jnp.float32,
                )
                parts = [s[:, n * BLK : (n + 1) * BLK] for n in range(6)]
                scores.append([t if n == 1 else t + bias[n] for n, t in enumerate(parts)])
            weights = []
            for parts in scores:
                top = jnp.max(functools.reduce(jnp.maximum, parts), axis=1, keepdims=True)
                top = jnp.broadcast_to(top * scale2, (BLK, BLK))
                weights.append([jnp.exp2(t * scale2 - top).astype(jnp.bfloat16) for t in parts])
            results = []
            for cols, parts in zip(columns, weights):
                values = [jnp.concatenate([x, ones], axis=1) for x in neighbours(1, b, cols)]
                total = jnp.dot(
                    jnp.concatenate(parts, axis=1),
                    jnp.concatenate(values, axis=0),
                    preferred_element_type=jnp.float32,
                )
                results.append((total[:, :HEAD_DIM] / total[:, HEAD_DIM:]).astype(out_ref.dtype))
            for cols, result in zip(columns, results):
                out_ref[0, rows, cols] = result

        @pl.when(jnp.logical_not(flagged))
        def _():
            out_ref[0, rows, :] = cached_ref[0, rows, :]


def attend_frame(frame, q, k, v, cached, allowed, flags, side, halos, behind, out):
    frames, tokens, width = q.shape
    blocks = tokens // BLK
    group = math.gcd(width // HEAD_DIM, GROUP)
    gw = group * HEAD_DIM

    def whole(f):
        return pl.BlockSpec((1, tokens, gw), lambda g: (f, 0, g))

    def pair(f, n):
        return pl.BlockSpec((2, 1, n, gw), lambda g: (0, f, 0, g))

    smem = pl.BlockSpec(memory_space=pltpu.SMEM)
    args = [allowed, flags, side, q, cached, k, v]
    specs = [smem, smem, smem, whole(frame), whole(frame), whole(frame), whole(frame)]
    if frame > 0:
        args += [k, v]
        specs += [whole(frame - 1), whole(frame - 1)]
        rims = [halos[frame], halos[frame - 1]]
    else:
        prev, prev_rims = behind
        args.append(prev)
        specs.append(pair(0, tokens))
        rims = [halos[frame], prev_rims]
    for left, right, relay, place in rims:
        arrived = [left, right] if relay is None else [left, right, relay]
        args += arrived
        specs += [pair(place, BLK)] * len(arrived)
    relayed = tuple(rim[2] is not None for rim in rims)
    aliases = {}
    if out is not None:
        aliases = {len(args): 0}
        args.append(out)
        specs.append(pl.BlockSpec(memory_space=pl.ANY))
    work = 4 * tokens * 6 * BLK * width
    return pl.pallas_call(
        functools.partial(frame_body, frame, relayed, blocks, group),
        grid=(width // gw,),
        in_specs=specs,
        out_specs=whole(frame),
        out_shape=jax.ShapeDtypeStruct(q.shape, q.dtype),
        input_output_aliases=aliases,
        compiler_params=pltpu.CompilerParams(vmem_limit_bytes=63 << 20),
        cost_estimate=pl.CostEstimate(
            flops=4 * work, bytes_accessed=12 * tokens * width * 2, transcendentals=0
        ),
        name=f"attend_frame_{frame}",
    )(*args)


def local(q, k, v, cached, pattern, refresh):
    frames, tokens, width = q.shape
    blocks = tokens // BLK
    last = frames - 1

    frame_at = lax.axis_index("frame") * frames + jnp.arange(frames, dtype=jnp.int32)
    block_at = lax.axis_index("tile") * blocks + jnp.arange(blocks, dtype=jnp.int32)
    n = jnp.arange(6, dtype=jnp.int32)
    spatial = block_at[None, :, None] + (n % 3 - 1)[None, None, :]
    inside = (
        (frame_at[:, None, None] - (n // 3)[None, None, :] >= 0)
        & (spatial >= 0)
        & (spatial < blocks * lax.axis_size("tile"))
    )
    allowed = jnp.where(inside, pattern, 0).reshape(frames, blocks * 6)

    prev = shift(jnp.stack([k[last:], v[last:]]), "frame", 1)
    halos = [None] * frames
    half = max(frames // 2, 1)
    starts = list(range(0, frames, half))[::-1]
    for start in starts:
        stop = min(start + half, frames)
        tail = jnp.stack([k[start:stop, tokens - BLK :], v[start:stop, tokens - BLK :]])
        head = jnp.stack([k[start:stop, :BLK], v[start:stop, :BLK]])
        if start == 0:
            left, right, relay = relayed_rims(tail, head)
        else:
            left, right, relay = shift(tail, "tile", 1), shift(head, "tile", -1), None
        for f in range(start, stop):
            halos[f] = (left, right, relay, f - start)
    prev_left = shift(prev[:, :, tokens - BLK :], "tile", 1)
    prev_right = shift(prev[:, :, :BLK], "tile", -1)
    behind = (prev, (prev_left, prev_right, None, 0))

    place = lax.axis_index("tile") % ROW
    side = jnp.stack([place == 0, place == ROW - 1]).astype(jnp.int32)
    out = None
    for frame in range(frames - 1, -1, -1):
        out = attend_frame(frame, q, k, v, cached, allowed, refresh, side, halos, behind, out)
    return out


def solution(mesh):
    wide = P("frame", "tile", None)
    return jax.shard_map(
        local,
        mesh=mesh,
        in_specs=(wide, wide, wide, wide, wide, P("frame", "tile")),
        out_specs=wide,
        check_vma=False,
    )
```
